32 devices in a mesh: dp: 8 (over y, x, core), tensor: 4 (over z).
Axes of the slice: x: 2, y: 2, z: 4, core: 2. Of those that a mesh axis runs over, the one named last changes fastest.
Arguments:
- latent: bfloat16 [4608, 512], P('dp'), may hold values from -6 to 6
- q_nope: bfloat16 [4608, 2048], P('dp', 'tensor'), may hold values from -6 to 6
- q_rope: bfloat16 [4608, 1024], P('dp', 'tensor'), may hold values from -40 to 40
- k_rope: bfloat16 [4608, 64], P('dp'), may hold values from -4.5 to 4.5
- grad_out: bfloat16 [4608, 2048], P('dp', 'tensor'), may hold values from -6 to 6
- offsets: int32 [8], P('dp'), may hold values from 1 to 575
- weight: bfloat16 [256, 16, 512], P(None, 'tensor'), may hold values from -0.25 to 0.25
- basis: float32 [512, 512], replicated, may hold values from -1 to 1
- first_moment: float32 [256, 16, 512], P('dp', 'tensor'), may hold values from -30 to 30
- second_rot: float32 [256, 16, 512], P('dp', 'tensor'), may hold values from 1 to 400
- second_plain: float32 [256, 16, 512], P('dp', 'tensor'), may hold values from 1 to 400
Outputs:
- grad_latent: bfloat16 [4608, 512], P(('dp', 'tensor'))
- new_weight: bfloat16 [256, 16, 512], P(None, 'tensor')
- new_first: float32 [256, 16, 512], P('dp', 'tensor')
- new_second: float32 [256, 16, 512], P('dp', 'tensor')
- new_plain: float32 [256, 16, 512], P('dp', 'tensor')
The draws below stay inside these ranges and needn't reach their ends.
All inputs are finite; a program needn't handle non-finite values.
Results may differ from the reference program's by a relative error of at most 0.011.
Values may be sent and summed in bfloat16 or wider, within the bound.
No kernel may reach another device: no remote copies, remote signals or barrier semaphores. Data moves between devices by JAX's collectives and lax.ppermute only.
A program may use at most 64 MiB of HBM per device.

```python
import math
import jax
import jax.numpy as jnp
from jax import lax

LAT = 512
HD = 128
ROPE = 64
SEQ = 576
HEADS = 16
GROUPS = 8
TOKENS = 4608


def rope_pair(key):
    key_query = jax.random.fold_in(key, 11)
    key_keys = jax.random.fold_in(key, 12)
    key_rope = jnp.clip(jax.random.normal(key_keys, (GROUPS, SEQ, ROPE), jnp.float32), -4.5, 4.5)
    query_rope = jnp.clip(jax.random.normal(key_query, (GROUPS, SEQ, HEADS, ROPE), jnp.float32), -6.0, 6.0)
    return (query_rope.reshape(GROUPS * SEQ, HEADS * ROPE), key_rope.reshape(GROUPS * SEQ, ROPE))


def draw_q_rope(key, part):
    return rope_pair(key)[0].astype(jnp.bfloat16)


def draw_k_rope(key, part):
    return rope_pair(key)[1].astype(jnp.bfloat16)


def draw_basis(key, part):
    highest = lax.Precision.HIGHEST
    jitter_terms = jax.random.normal(jax.random.fold_in(key, 21), (LAT, LAT), jnp.float32) * (0.6 / LAT ** 0.5)
    matrix = (jnp.eye(LAT, dtype=jnp.float32) + jitter_terms) / 1.7
    for _ in range(16):
        square = jnp.dot(matrix, matrix.T, precision=highest)
        matrix = 1.5 * matrix - 0.5 * jnp.dot(square, matrix, precision=highest)
    return jnp.clip(matrix, -1.0, 1.0)


def place_ends(values, stream_key, low, high):
    dims = values.shape
    index_at = [jax.random.randint(jax.random.fold_in(stream_key, axis), (), 0, dims[axis]) for axis in range(len(dims))]
    values = values.at[tuple(index_at)].set(low)
    longest = dims.index(max(dims))
    index_at[longest] = (index_at[longest] + 1) % dims[longest]
    return values.at[tuple(index_at)].set(high)


def steps_of(own_key, extent, split, least, top_value):
    loudness = 1.0
    for dim, blocks in split:
        steps = jax.random.uniform(jax.random.fold_in(jax.random.fold_in(own_key, 6), dim), (blocks,), jnp.float32, least / len(split), top_value / len(split))
        loudness = loudness * jnp.repeat(jnp.exp(steps), extent[dim] // blocks).reshape((-1,) + (1,) * (len(extent) - 1 - dim))
    return loudness


def noise(rng, dims, scale, limit, split=(), kind=jnp.bfloat16):
    values = scale * jax.random.normal(rng, dims, jnp.float32)
    if split:
        values = values * steps_of(rng, dims, split, -0.22, 0.18)
    return jnp.clip(values, -limit, limit).astype(kind)


def setup_inputs(seed: int = 0) -> dict:
    key_of = jax.random.split(jax.random.key(seed), 12)
    return {
        "latent": noise(key_of[0], (TOKENS, LAT), 1.0, 6.0, ((0, 8),)),
        "q_nope": noise(key_of[1], (TOKENS, HEADS * HD), 1.0, 6.0, ((0, 8), (1, 4))),
        "q_rope": draw_q_rope(jax.random.fold_in(key_of[11], 71), 0),
        "k_rope": draw_k_rope(jax.random.fold_in(key_of[11], 71), 0),
        "grad_out": noise(key_of[4], (TOKENS, HEADS * HD), 1.0, 6.0, ((0, 8), (1, 4))),
        "offsets": place_ends(jax.random.randint(key_of[5], (GROUPS,), 1, SEQ), jax.random.fold_in(key_of[5], 1), 1, SEQ - 1).astype(jnp.int32),
        "weight": noise(key_of[6], (2 * HD, HEADS, LAT), LAT ** -0.5, 0.25, ((1, 4),)),
        "basis": draw_basis(jax.random.fold_in(key_of[11], 71), 0),
        "first_moment": noise(key_of[8], (2 * HD, HEADS, LAT), 5.0, 30.0, ((0, 8), (1, 4)), jnp.float32),
        "second_rot": jnp.clip(jnp.exp(math.log(400.0) - 5.9914645 * jax.random.uniform(key_of[9], (2 * HD, HEADS, LAT), jnp.float32) ** steps_of(key_of[9], (2 * HD, HEADS, LAT), ((0, 8), (1, 4)), -0.2, 0.2)), 1.0, 400.0),
        "second_plain": jnp.clip(jnp.exp(math.log(400.0) - 5.9914645 * jax.random.uniform(key_of[10], (2 * HD, HEADS, LAT), jnp.float32) ** steps_of(key_of[10], (2 * HD, HEADS, LAT), ((0, 8), (1, 4)), -0.2, 0.2)), 1.0, 400.0),
    }


beta_first = 0.9
beta_second = 0.95
epsilon = 1e-08
learn_rate = 0.002
decay_rate = 0.1
blend_share = 0.5

def group_pass(weight, latent, q_nope, q_rope, k_rope, grad_out, offset):
    f32 = jnp.float32
    score_scale = float(HD + ROPE) ** (-0.5)
    key_value = jnp.einsum('tc,rhc->thr', latent.astype(f32), weight.astype(f32)).astype(jnp.bfloat16)
    keys = key_value[:, :, :HD].astype(f32)
    values = key_value[:, :, HD:].astype(f32)
    query_main = q_nope.reshape(SEQ, HEADS, HD).astype(f32)
    query_side = q_rope.reshape(SEQ, HEADS, ROPE).astype(f32)
    out_grads = grad_out.reshape(SEQ, HEADS, HD).astype(f32)
    scores = (jnp.einsum('ihd,jhd->hij', query_main, keys) + jnp.einsum('ihe,je->hij', query_side, k_rope.astype(f32))) * score_scale
    positions = jnp.arange(SEQ, dtype=jnp.int32)
    visible = positions[None, :] <= jnp.maximum(positions[:, None], offset - 1)
    masked = jnp.where(visible[None], scores, -jnp.inf)
    row_max = lax.optimization_barrier(jnp.max(masked, axis=-1, keepdims=True))
    exp_terms = jnp.where(visible[None], jnp.exp(masked - row_max), 0.0)
    attn_probs = exp_terms / lax.optimization_barrier(jnp.sum(exp_terms, axis=-1, keepdims=True))
    probs_low = attn_probs.astype(jnp.bfloat16).astype(f32)
    attended = jnp.einsum('hij,jhd->ihd', probs_low, values)
    row_delta = lax.optimization_barrier(jnp.sum(out_grads * attended, axis=-1))
    grad_probs = jnp.einsum('ihd,jhd->hij', out_grads, values)
    grad_scores = (attn_probs * (grad_probs - jnp.transpose(row_delta)[:, :, None]) * score_scale).astype(jnp.bfloat16).astype(f32)
    grad_keys = jnp.einsum('hij,ihd->jhd', grad_scores, query_main)
    grad_values = jnp.einsum('hij,ihd->jhd', probs_low, out_grads)
    grad_kv = jnp.concatenate([grad_keys, grad_values], axis=-1).astype(jnp.bfloat16).astype(f32)
    grad_latent = jnp.einsum('thr,rhc->tc', grad_kv, weight.astype(f32)).astype(jnp.bfloat16)
    weight_part = jnp.einsum('thr,tc->rhc', grad_kv, latent.astype(f32))
    return (grad_latent, weight_part)

def reference(latent, q_nope, q_rope, k_rope, grad_out, offsets, weight, basis, first_moment, second_rot, second_plain):
    f32 = jnp.float32
    highest = lax.Precision.HIGHEST
    stacked = (latent.reshape(GROUPS, SEQ, LAT), q_nope.reshape(GROUPS, SEQ, HEADS * HD), q_rope.reshape(GROUPS, SEQ, HEADS * ROPE), k_rope.reshape(GROUPS, SEQ, ROPE), grad_out.reshape(GROUPS, SEQ, HEADS * HD), offsets)

    def step_group(carry, inputs):
        grad_latent, weight_part = group_pass(weight, inputs[0], inputs[1], inputs[2], inputs[3], inputs[4], inputs[5])
        return (carry + weight_part, grad_latent)
    weight_grad, latent_parts = lax.scan(step_group, jnp.zeros((2 * HD, HEADS, LAT), f32), stacked)
    grad_latent = latent_parts.reshape(TOKENS, LAT)
    rotated = jnp.einsum('rhc,ce->rhe', weight_grad, basis, precision=highest)
    new_first = beta_first * first_moment + (1.0 - beta_first) * rotated
    new_second = beta_second * second_rot + (1.0 - beta_second) * rotated * rotated
    new_plain = beta_second * second_plain + (1.0 - beta_second) * weight_grad * weight_grad
    soap_part = jnp.einsum('rhe,ce->rhc', new_first / (jnp.sqrt(new_second) + epsilon), basis, precision=highest)
    back_moment = jnp.einsum('rhe,ce->rhc', new_first, basis, precision=highest)
    direction = blend_share * soap_part + blend_share * back_moment / (jnp.sqrt(new_plain) + epsilon)
    old_weight = weight.astype(f32)
    new_weight = (old_weight - learn_rate * (direction + decay_rate * old_weight)).astype(jnp.bfloat16)
    return (grad_latent, new_weight, new_first, new_second, new_plain)
```

```python
import functools

import jax
import jax.numpy as jnp
from jax import lax
from jax.experimental import pallas as pl
from jax.experimental.pallas import tpu as pltpu
from jax.sharding import PartitionSpec as P

beta_first = 0.9
beta_second = 0.95
epsilon = 1e-08
learn_rate = 0.002
decay_rate = 0.1
blend_share = 0.5
log2_e = 1.4426950408889634
f32 = jnp.float32
bf16 = jnp.bfloat16
VMEM = pl.BlockSpec(memory_space=pltpu.VMEM)
SMEM = pl.BlockSpec(memory_space=pltpu.SMEM)


def mm(a, b):
    return lax.dot_general(a, b, (((1,), (0,)), ((), ())), preferred_element_type=f32)


def mm_nt(a, b):
    return lax.dot_general(a, b, (((1,), (1,)), ((), ())), preferred_element_type=f32)


def mm_tn(a, b):
    return lax.dot_general(a, b, (((0,), (0,)), ((), ())), preferred_element_type=f32)


def attend_kernel(
    ids, offsets, latent, q_nope, q_rope, k_rope, grad_out, weight, keep, send, glat, key_value, grad_kv, slab
):
    seq_len, latent_dim = latent.shape
    heads, width, _ = weight.shape
    head_dim = width // 2
    rope_dim = k_rope.shape[1]
    chips = keep.shape[0]
    rows = width // (2 * chips)
    parts = glat.shape[0]
    part_rows = seq_len // parts
    scale = float(head_dim + rope_dim) ** (-0.5)
    lat = latent[...]
    wall = weight[...].reshape(heads * width, latent_dim)
    key_value[...] = mm_nt(lat, wall).astype(bf16)
    limit = jnp.maximum(lax.broadcasted_iota(jnp.int32, (1, seq_len), 1), offsets[0] - 1)
    visible = lax.broadcasted_iota(jnp.int32, (seq_len, seq_len), 0) <= limit
    for h in range(heads):
        q_main = q_nope[:, h * head_dim : (h + 1) * head_dim]
        g_out = grad_out[:, h * head_dim : (h + 1) * head_dim]
        q_all = jnp.concatenate([q_main, q_rope[:, h * rope_dim : (h + 1) * rope_dim]], axis=1)
        keys = key_value[:, h * width : h * width + head_dim]
        values = key_value[:, h * width + head_dim : (h + 1) * width]
        k_all = jnp.concatenate([keys, k_rope[...]], axis=1)
        scores = jnp.where(visible, mm_nt(k_all, q_all), -1e30)
        top = jnp.max(scores, axis=0, keepdims=True)
        terms = jnp.exp2((scores - top) * (scale * log2_e))
        inv = 1.0 / jnp.sum(terms, axis=0, keepdims=True)
        probs = terms * inv
        grad_probs = mm_nt(values, g_out)
        delta = jnp.sum(probs * grad_probs, axis=0, keepdims=True)
        grad_scores = (probs * (grad_probs - delta) * scale).astype(bf16)
        grad_kv[:, h * width : h * width + head_dim] = mm(grad_scores, q_main).astype(bf16)
        grad_kv[:, h * width + head_dim : (h + 1) * width] = mm(probs.astype(bf16), g_out).astype(bf16)
    gkv = grad_kv[...]
    slab[...] = mm_tn(gkv, lat).reshape(heads, 2 * chips, rows, latent_dim)
    my_chip, my_core, my_part = ids[0], ids[1], ids[2]
    for k in range(chips):
        chip = lax.rem(my_chip + k, chips) if chips & (chips - 1) else my_chip ^ k
        mine, other = 2 * chip + my_core, 2 * chip + 1 - my_core
        for h in range(heads):
            keep[k, h * rows : (h + 1) * rows, :] = slab[h, mine].astype(bf16)
            send[k, h * rows : (h + 1) * rows, :] = slab[h, other].astype(bf16)
    gl = mm(gkv, wall).astype(bf16)
    for s in range(parts):
        to = lax.rem(s - my_part + parts, parts)
        glat[to] = gl[s * part_rows : (s + 1) * part_rows, :]


def add_kernel(keep, came, *outs):
    for k, out in enumerate(outs):
        total = keep[k].astype(f32) + came[k].astype(f32)
        out[...] = total.astype(out.dtype)


def soap_kernel(ids, weight, basis, first_moment, second_rot, second_plain, *refs):
    slab_out, new_first, new_second, new_plain, direction, grad, stage = refs[-7:]
    parts = refs[:-7]
    rows, heads, latent_dim = first_moment.shape
    grad[...] = functools.reduce(jnp.add, [p[...].astype(f32) for p in parts])
    turn = basis[...].astype(bf16)
    rotated = mm(grad[...].astype(bf16), turn)
    start = (2 * ids[0] + ids[1]) * rows
    for h in range(heads):
        own = slice(h * rows, (h + 1) * rows)
        rot = rotated[own]
        moment = beta_first * first_moment[:, h, :] + (1.0 - beta_first) * rot
        rot_sq = beta_second * second_rot[:, h, :] + (1.0 - beta_second) * rot * rot
        new_first[:, h, :] = moment
        new_second[:, h, :] = rot_sq
        stage[own, :] = (moment / (jnp.sqrt(rot_sq) + epsilon)).astype(bf16)
        stage[(heads + h) * rows : (heads + h + 1) * rows, :] = moment.astype(bf16)
    turned = mm_nt(stage[...], turn)
    for h in range(heads):
        own = slice(h * rows, (h + 1) * rows)
        g = grad[own, :]
        plain = beta_second * second_plain[:, h, :] + (1.0 - beta_second) * g * g
        new_plain[:, h, :] = plain
        back = turned[(heads + h) * rows : (heads + h + 1) * rows]
        direction[:, h, :] = blend_share * turned[own] + blend_share * back / (jnp.sqrt(plain) + epsilon)
    old = weight[pl.ds(start, rows)].astype(f32)
    slab_out[...] = (old - learn_rate * (direction[...] + decay_rate * old)).astype(bf16)


def place_kernel(ids, *refs):
    out = refs[-1]
    rows = refs[0].shape[0]
    chips = (len(refs) - 1) // 2
    for k in range(chips):
        chip = lax.rem(ids[0] - k + chips, chips) if chips & (chips - 1) else ids[0] ^ k
        out[pl.ds((2 * chip + ids[1]) * rows, rows)] = refs[k][...]
        out[pl.ds((2 * chip + 1 - ids[1]) * rows, rows)] = refs[chips + k][...]


def local(latent, q_nope, q_rope, k_rope, grad_out, offsets, weight, basis, first_moment, second_rot, second_plain):
    seq_len, latent_dim = latent.shape
    width, heads, _ = weight.shape
    dp, parts = lax.axis_size("dp"), lax.axis_size("tensor")
    chips = dp // 2
    rows = width // dp
    part_rows = seq_len // parts
    me = lax.axis_index("dp")
    ids = jnp.stack([me // 2, me % 2, lax.axis_index("tensor")]).astype(jnp.int32)

    def core_swap(x):
        return lax.ppermute(x, "dp", [(i, i ^ 1) for i in range(dp)])

    def chip_move(x, k):
        if chips & (chips - 1):
            pairs = [(i, (i + 2 * k) % dp) for i in range(dp)]
        else:
            pairs = [(i, i ^ (2 * k)) for i in range(dp)]
        return lax.ppermute(x, "dp", pairs)

    def part_move(x, s):
        return lax.ppermute(x, "tensor", [(i, (i + s) % parts) for i in range(parts)])

    params = pltpu.CompilerParams(vmem_limit_bytes=40 * 1024 * 1024)
    keep, send, glat = pl.pallas_call(
        attend_kernel,
        out_shape=(
            jax.ShapeDtypeStruct((chips, heads * rows, latent_dim), bf16),
            jax.ShapeDtypeStruct((chips, heads * rows, latent_dim), bf16),
            jax.ShapeDtypeStruct((parts, part_rows, latent_dim), bf16),
        ),
        in_specs=[SMEM, SMEM] + [VMEM] * 6,
        out_specs=(VMEM, VMEM, VMEM),
        scratch_shapes=[
            pltpu.VMEM((seq_len, heads * width), bf16),
            pltpu.VMEM((seq_len, heads * width), bf16),
            pltpu.VMEM((heads, dp, rows, latent_dim), f32),
        ],
        compiler_params=params,
        name="attend",
    )(ids, offsets, latent, q_nope, q_rope, k_rope, grad_out, jnp.transpose(weight, (1, 0, 2)))

    came = core_swap(send)
    sums = pl.pallas_call(
        add_kernel,
        out_shape=[jax.ShapeDtypeStruct((heads * rows, latent_dim), f32 if k == 0 else bf16) for k in range(chips)],
        in_specs=[VMEM, VMEM],
        out_specs=[VMEM] * chips,
        name="pair_sum",
    )(keep, came)
    got = [sums[0]] + [chip_move(sums[k], k) for k in range(1, chips)]
    glat_parts = [glat[0]] + [part_move(glat[s], s) for s in range(1, parts)]

    state = jax.ShapeDtypeStruct((rows, heads, latent_dim), f32)
    stage_rows = heads * rows
    new_slab, new_first, new_second, new_plain = pl.pallas_call(
        soap_kernel,
        out_shape=(jax.ShapeDtypeStruct((rows, heads, latent_dim), bf16), state, state, state),
        in_specs=[SMEM] + [VMEM] * (5 + chips),
        out_specs=(VMEM,) * 4,
        scratch_shapes=[
            pltpu.VMEM((rows, heads, latent_dim), f32),
            pltpu.VMEM((stage_rows, latent_dim), f32),
            pltpu.VMEM((2 * stage_rows, latent_dim), bf16),
        ],
        compiler_params=params,
        name="soap",
    )(ids, weight, basis, first_moment, second_rot, second_plain, *got)

    mine = [new_slab] + [chip_move(new_slab, k) for k in range(1, chips)]
    others = [core_swap(x) for x in mine]
    new_weight = pl.pallas_call(
        place_kernel,
        out_shape=jax.ShapeDtypeStruct((width, heads, latent_dim), bf16),
        in_specs=[SMEM] + [VMEM] * (2 * chips),
        out_specs=VMEM,
        name="place",
    )(ids, *mine, *others)
    grad_latent = functools.reduce(jnp.add, [x.astype(f32) for x in glat_parts]).astype(bf16)
    return (grad_latent, new_weight, new_first, new_second, new_plain)


def solution(mesh):
    state = P("dp", "tensor", None)
    return jax.shard_map(
        local,
        mesh=mesh,
        in_specs=(
            P("dp", None),
            P("dp", "tensor"),
            P("dp", "tensor"),
            P("dp", None),
            P("dp", "tensor"),
            P("dp"),
            P(None, "tensor", None),
            P(),
            state,
            state,
            state,
        ),
        out_specs=(P(("dp", "tensor"), None), P(None, "tensor", None), state, state, state),
        check_vma=False,
    )
```

```python
import functools

import jax
import jax.numpy as jnp
from jax import lax
from jax.experimental import pallas as pl
from jax.experimental.pallas import tpu as pltpu
from jax.sharding import PartitionSpec as P

beta_first = 0.9
beta_second = 0.95
epsilon = 1e-08
learn_rate = 0.002
decay_rate = 0.1
blend_share = 0.5
log2_e = 1.4426950408889634
f32 = jnp.float32
bf16 = jnp.bfloat16
in_vmem = pl.BlockSpec(memory_space=pltpu.VMEM)
in_hbm = pl.BlockSpec(memory_space=pltpu.HBM)


def mm(a, b):
    return lax.dot_general(a, b, (((1,), (0,)), ((), ())), preferred_element_type=f32)


def mm_nt(a, b):
    return lax.dot_general(a, b, (((1,), (1,)), ((), ())), preferred_element_type=f32)


def mm_tn(a, b):
    return lax.dot_general(a, b, (((0,), (0,)), ((), ())), preferred_element_type=f32)


def limit_mib(mib):
    return pltpu.CompilerParams(vmem_limit_bytes=mib * 1024 * 1024)


def other_chip(chip, k, chips):
    return lax.rem(chip + k, chips) if chips & (chips - 1) else chip ^ k


def sender_chip(chip, k, chips):
    return lax.rem(chip - k + chips, chips) if chips & (chips - 1) else chip ^ k


def place_of():
    me = lax.axis_index("dp")
    return lax.div(me, 2), lax.rem(me, 2)


def attend_kernel(
    offsets,
    latent,
    q_nope,
    q_rope,
    k_rope_t,
    grad_out,
    weight,
    basis,
    first_moment,
    second_rot,
    second_plain,
    send,
    keep,
    grad_kv,
    wall,
    own_weight,
    basis_v,
    first_v,
    rot_v,
    plain_v,
    lat,
    q_main_v,
    q_side_v,
    k_side_v,
    g_out_v,
    weight_v,
    key_value,
    slab,
    sems,
):
    seq_len, latent_dim = latent.shape
    width, heads, _ = weight.shape
    head_dim = width // 2
    rope_dim = k_rope_t.shape[0]
    chips, _, rows, _ = keep.shape
    scale = float(head_dim + rope_dim) ** (-0.5)
    pairs = [
        (weight, weight_v),
        (latent, lat),
        (k_rope_t, k_side_v),
        (q_nope, q_main_v),
        (q_rope, q_side_v),
        (grad_out, g_out_v),
        (basis, basis_v),
        (first_moment, first_v),
        (second_rot, rot_v),
        (second_plain, plain_v),
    ]
    copies = [pltpu.make_async_copy(a, b, sems.at[i]) for i, (a, b) in enumerate(pairs)]
    for copy in copies:
        copy.start()
    limit = jnp.maximum(lax.broadcasted_iota(jnp.int32, (1, seq_len), 1), offsets[0] - 1)
    visible = lax.broadcasted_iota(jnp.int32, (seq_len, seq_len), 0) <= limit
    copies[0].wait()
    wall[...] = jnp.swapaxes(weight_v[...], 0, 1).reshape(heads * width, latent_dim)
    copies[1].wait()
    key_value[...] = mm_nt(lat[...], wall[...]).astype(bf16)
    for copy in copies[2:6]:
        copy.wait()
    k_side = k_side_v[...].T
    for h in range(heads):
        q_main = q_main_v[:, h * head_dim : (h + 1) * head_dim]
        g_out = g_out_v[:, h * head_dim : (h + 1) * head_dim]
        q_all = jnp.concatenate([q_main, q_side_v[:, h * rope_dim : (h + 1) * rope_dim]], axis=1)
        keys = key_value[:, h * width : h * width + head_dim]
        values = key_value[:, h * width + head_dim : (h + 1) * width]
        k_all = jnp.concatenate([keys, k_side], axis=1)
        scores = jnp.where(visible, mm_nt(k_all, q_all), -1e30)
        top = jnp.max(scores, axis=0, keepdims=True)
        terms = jnp.exp2((scores - top) * (scale * log2_e))
        inv = 1.0 / jnp.sum(terms, axis=0, keepdims=True)
        probs = terms * inv
        grad_probs = mm_nt(values, g_out)
        delta = jnp.sum(probs * grad_probs, axis=0, keepdims=True)
        grad_scores = (probs * (grad_probs - delta) * scale).astype(bf16)
        grad_kv[:, h * width : h * width + head_dim] = mm(grad_scores, q_main).astype(bf16)
        grad_kv[:, h * width + head_dim : (h + 1) * width] = mm(probs.astype(bf16), g_out).astype(bf16)
    slab[...] = mm_tn(grad_kv[...], lat[...]).reshape(heads, 2 * chips, rows, latent_dim)
    my_chip, my_core = place_of()
    for k in range(chips):
        chip = other_chip(my_chip, k, chips)
        for h in range(heads):
            send[k, h] = slab[h, 2 * chip + 1 - my_core].astype(bf16)
            keep[k, h] = slab[h, 2 * chip + my_core].astype(bf16)
    own_weight[...] = weight_v[pl.ds((2 * my_chip + my_core) * rows, rows)]
    for copy in copies[6:]:
        copy.wait()


def latent_kernel(grad_kv, wall, basis, *refs):
    turn, total, outs = refs[0], refs[-1], refs[1:-1]
    parts = len(outs)
    total[...] = mm(grad_kv[...], wall[...]).astype(bf16).reshape(total.shape)
    for s, out in enumerate(outs):
        out[...] = total[lax.rem(lax.axis_index("tensor") + s, parts)]
    turn[...] = basis[...].astype(bf16)


def pair_kernel(keep, came, *outs):
    for k, out in enumerate(outs):
        out[...] = (keep[k].astype(f32) + came[k].astype(f32)).astype(out.dtype)


def soap_kernel(old, turn, first_moment, second_rot, second_plain, *refs):
    parts, (slab_out, new_first, new_second, new_plain) = refs[:-4], refs[-4:]
    rows, heads, latent_dim = first_moment.shape
    flat = (heads * rows, latent_dim)

    def by_head(x):
        return jnp.swapaxes(x, 0, 1).reshape(flat)

    def by_row(x):
        return jnp.swapaxes(x.reshape(heads, rows, latent_dim), 0, 1)

    grad = functools.reduce(jnp.add, [p[...].astype(f32) for p in parts]).reshape(flat)
    rotated = mm(grad.astype(bf16), turn[...])
    moment = beta_first * by_head(first_moment[...]) + (1.0 - beta_first) * rotated
    rot_sq = beta_second * by_head(second_rot[...]) + (1.0 - beta_second) * rotated * rotated
    plain_sq = beta_second * by_head(second_plain[...]) + (1.0 - beta_second) * grad * grad
    stacked = jnp.concatenate([moment / (jnp.sqrt(rot_sq) + epsilon), moment], axis=0).astype(bf16)
    turned = mm_nt(stacked, turn[...])
    direction = blend_share * turned[: flat[0]] + blend_share * turned[flat[0] :] / (jnp.sqrt(plain_sq) + epsilon)
    before = old[...].astype(f32)
    slab_out[...] = (before - learn_rate * (by_row(direction) + decay_rate * before)).astype(bf16)
    new_first[...] = by_row(moment)
    new_second[...] = by_row(rot_sq)
    new_plain[...] = by_row(plain_sq)


def place_kernel(*refs):
    chips = (len(refs) - 2) // 2
    out, sems = refs[-2:]
    rows = refs[0].shape[0]
    my_chip, my_core = place_of()
    copies = []
    for k in range(chips):
        chip = sender_chip(my_chip, k, chips)
        for side in range(2):
            core = my_core if side == 0 else 1 - my_core
            spot = out.at[pl.ds((2 * chip + core) * rows, rows)]
            copies.append(pltpu.make_async_copy(refs[side * chips + k], spot, sems.at[2 * k + side]))
    for copy in copies:
        copy.start()
    for copy in copies:
        copy.wait()


def part_sum_kernel(*refs):
    refs[-1][...] = functools.reduce(jnp.add, [x[...].astype(f32) for x in refs[:-1]]).astype(bf16)


def local(latent, q_nope, q_rope, k_rope, grad_out, offsets, weight, basis, first_moment, second_rot, second_plain):
    seq_len, latent_dim = latent.shape
    width, heads, _ = weight.shape
    dp, parts = lax.axis_size("dp"), lax.axis_size("tensor")
    chips = dp // 2
    rows = width // dp
    part_rows = seq_len // parts
    rope_dim = k_rope.shape[1]

    def core_swap(x):
        return lax.ppermute(x, "dp", [(i, i ^ 1) for i in range(dp)])

    def chip_move(x, k):
        if chips & (chips - 1):
            pairs = [(i, (i + 2 * k) % dp) for i in range(dp)]
        else:
            pairs = [(i, i ^ (2 * k)) for i in range(dp)]
        return lax.ppermute(x, "dp", pairs)

    def part_move(x, s):
        return lax.ppermute(x, "tensor", [(i, (i + s) % parts) for i in range(parts)])

    piece = (heads, rows, latent_dim)
    state = (rows, heads, latent_dim)
    send, keep, grad_kv, wall, own_weight, basis_v, first_v, rot_v, plain_v = pl.pallas_call(
        attend_kernel,
        out_shape=(
            pltpu.VMEM((chips,) + piece, bf16),
            pltpu.VMEM((chips,) + piece, bf16),
            pltpu.VMEM((seq_len, heads * width), bf16),
            pltpu.VMEM((heads * width, latent_dim), bf16),
            pltpu.VMEM(state, bf16),
            pltpu.VMEM(basis.shape, f32),
            pltpu.VMEM(state, f32),
            pltpu.VMEM(state, f32),
            pltpu.VMEM(state, f32),
        ),
        in_specs=[pl.BlockSpec(memory_space=pltpu.SMEM)] + [in_hbm] * 10,
        out_specs=(in_vmem,) * 9,
        scratch_shapes=[
            pltpu.VMEM(latent.shape, bf16),
            pltpu.VMEM(q_nope.shape, bf16),
            pltpu.VMEM(q_rope.shape, bf16),
            pltpu.VMEM((rope_dim, seq_len), bf16),
            pltpu.VMEM(grad_out.shape, bf16),
            pltpu.VMEM(weight.shape, bf16),
            pltpu.VMEM((seq_len, heads * width), bf16),
            pltpu.VMEM((heads, dp, rows, latent_dim), f32),
            pltpu.SemaphoreType.DMA((10,)),
        ],
        compiler_params=limit_mib(32),
        name="attend",
    )(offsets, *[
        pltpu.with_memory_space_constraint(x, pltpu.HBM)
        for x in (
            latent, q_nope, q_rope, k_rope.T, grad_out, weight, basis, first_moment, second_rot, second_plain
        )
    ])

    came = core_swap(send)
    turn, *glat = pl.pallas_call(
        latent_kernel,
        out_shape=[pltpu.VMEM(basis.shape, bf16)] + [pltpu.VMEM((part_rows, latent_dim), bf16)] * parts,
        in_specs=[in_vmem] * 3,
        out_specs=[in_vmem] * (1 + parts),
        scratch_shapes=[pltpu.VMEM((parts, part_rows, latent_dim), bf16)],
        compiler_params=limit_mib(8),
        name="latent_share",
    )(grad_kv, wall, basis_v)
    sums = pl.pallas_call(
        pair_kernel,
        out_shape=[pltpu.VMEM(piece, f32 if k == 0 else bf16) for k in range(chips)],
        in_specs=[in_vmem] * 2,
        out_specs=[in_vmem] * chips,
        compiler_params=limit_mib(4),
        name="pair_sum",
    )(keep, came)
    sums, glat = lax.optimization_barrier((sums, glat))
    got = [sums[0]] + [chip_move(sums[k], k) for k in range(1, chips)]
    glat = [glat[0]] + [part_move(glat[s], s) for s in range(1, parts)]

    new_slab, new_first, new_second, new_plain = pl.pallas_call(
        soap_kernel,
        out_shape=(pltpu.VMEM(state, bf16),) + (pltpu.VMEM(state, f32),) * 3,
        in_specs=[in_vmem] * (5 + chips),
        out_specs=(in_vmem,) * 4,
        compiler_params=limit_mib(8),
        name="soap",
    )(own_weight, turn, first_v, rot_v, plain_v, *got)

    mine = [new_slab] + [chip_move(new_slab, k) for k in range(1, chips)]
    others = [core_swap(x) for x in mine]
    grad_latent = pl.pallas_call(
        part_sum_kernel,
        out_shape=jax.ShapeDtypeStruct((part_rows, latent_dim), bf16),
        in_specs=[in_vmem] * parts,
        out_specs=in_vmem,
        compiler_params=limit_mib(4),
        name="part_sum",
    )(*glat)
    new_weight = pl.pallas_call(
        place_kernel,
        out_shape=pltpu.HBM((width, heads, latent_dim), bf16),
        in_specs=[in_vmem] * (2 * chips),
        out_specs=in_hbm,
        scratch_shapes=[pltpu.SemaphoreType.DMA((2 * chips,))],
        compiler_params=limit_mib(4),
        name="place",
    )(*mine, *others)
    return (grad_latent, new_weight, new_first, new_second, new_plain)


def solution(mesh):
    state = P("dp", "tensor", None)
    return jax.shard_map(
        local,
        mesh=mesh,
        in_specs=(
            P("dp", None),
            P("dp", "tensor"),
            P("dp", "tensor"),
            P("dp", None),
            P("dp", "tensor"),
            P("dp"),
            P(None, "tensor", None),
            P(),
            state,
            state,
            state,
        ),
        out_specs=(P(("dp", "tensor"), None), P(None, "tensor", None), state, state, state),
        check_vma=False,
    )
```

```python
import functools

import jax
import jax.numpy as jnp
from jax import lax
from jax.experimental import pallas as pl
from jax.experimental.pallas import tpu as pltpu
from jax.sharding import PartitionSpec as P

beta_first = 0.9
beta_second = 0.95
epsilon = 1e-08
learn_rate = 0.002
decay_rate = 0.1
blend_share = 0.5
log2_e = 1.4426950408889634
f32 = jnp.float32
bf16 = jnp.bfloat16
in_vmem = pl.BlockSpec(memory_space=pltpu.VMEM)
in_hbm = pl.BlockSpec(memory_space=pltpu.HBM)


def mm(a, b):
    return lax.dot_general(a, b, (((1,), (0,)), ((), ())), preferred_element_type=f32)


def mm_nt(a, b):
    return lax.dot_general(a, b, (((1,), (1,)), ((), ())), preferred_element_type=f32)


def mm_tn(a, b):
    return lax.dot_general(a, b, (((0,), (0,)), ((), ())), preferred_element_type=f32)


def limit_mib(mib):
    return pltpu.CompilerParams(vmem_limit_bytes=mib * 1024 * 1024)


def other_chip(chip, k, chips):
    return lax.rem(chip + k, chips) if chips & (chips - 1) else chip ^ k


def sender_chip(chip, k, chips):
    return lax.rem(chip - k + chips, chips) if chips & (chips - 1) else chip ^ k


def place_of():
    me = lax.axis_index("dp")
    return lax.div(me, 2), lax.rem(me, 2)


def attend_kernel(
    offsets,
    latent,
    q_nope,
    q_rope,
    k_rope_t,
    grad_out,
    weight,
    send,
    keep,
    grad_kv,
    wall,
    own_weight,
    lat,
    q_main_v,
    q_side_v,
    k_side_v,
    g_out_v,
    weight_v,
    key_value,
    slab,
    sems,
):
    seq_len, latent_dim = latent.shape
    width, heads, _ = weight.shape
    head_dim = width // 2
    rope_dim = k_rope_t.shape[0]
    chips, _, rows, _ = keep.shape
    scale = float(head_dim + rope_dim) ** (-0.5)
    pairs = [
        (weight, weight_v),
        (latent, lat),
        (k_rope_t, k_side_v),
        (q_nope, q_main_v),
        (q_rope, q_side_v),
        (grad_out, g_out_v),
    ]
    copies = [pltpu.make_async_copy(a, b, sems.at[i]) for i, (a, b) in enumerate(pairs)]
    for copy in copies:
        copy.start()
    limit = jnp.maximum(lax.broadcasted_iota(jnp.int32, (1, seq_len), 1), offsets[:1, :1] - 1)
    visible = lax.broadcasted_iota(jnp.int32, (seq_len, seq_len), 0) <= limit
    copies[0].wait()
    wall[...] = jnp.swapaxes(weight_v[...], 0, 1).reshape(heads * width, latent_dim)
    copies[1].wait()
    key_value[...] = mm_nt(lat[...], wall[...]).astype(bf16)
    for copy in copies[2:6]:
        copy.wait()
    k_side = k_side_v[...].T
    for h in range(heads):
        q_main = q_main_v[:, h * head_dim : (h + 1) * head_dim]
        g_out = g_out_v[:, h * head_dim : (h + 1) * head_dim]
        q_all = jnp.concatenate([q_main, q_side_v[:, h * rope_dim : (h + 1) * rope_dim]], axis=1)
        keys = key_value[:, h * width : h * width + head_dim]
        values = key_value[:, h * width + head_dim : (h + 1) * width]
        k_all = jnp.concatenate([keys, k_side], axis=1)
        scores = jnp.where(visible, mm_nt(k_all, q_all), -1e30)
        top = jnp.max(scores, axis=0, keepdims=True)
        terms = jnp.exp2((scores - top) * (scale * log2_e))
        inv = 1.0 / jnp.sum(terms, axis=0, keepdims=True)
        probs = terms * inv
        grad_probs = mm_nt(values, g_out)
        delta = jnp.sum(probs * grad_probs, axis=0, keepdims=True)
        grad_scores = (probs * (grad_probs - delta) * scale).astype(bf16)
        grad_kv[:, h * width : h * width + head_dim] = mm(grad_scores, q_main).astype(bf16)
        grad_kv[:, h * width + head_dim : (h + 1) * width] = mm(probs.astype(bf16), g_out).astype(bf16)
    slab[...] = mm_tn(grad_kv[...], lat[...]).reshape(heads, 2 * chips, rows, latent_dim)
    my_chip, my_core = place_of()
    for k in range(chips):
        chip = other_chip(my_chip, k, chips)
        for h in range(heads):
            send[k, h] = slab[h, 2 * chip + 1 - my_core].astype(bf16)
            keep[k, h] = slab[h, 2 * chip + my_core].astype(bf16)
    own_weight[...] = weight_v[pl.ds((2 * my_chip + my_core) * rows, rows)]


def latent_kernel(grad_kv, wall, *refs):
    total, outs = refs[-1], refs[:-1]
    parts = len(outs)
    total[...] = mm(grad_kv[...], wall[...]).astype(bf16).reshape(total.shape)
    for s, out in enumerate(outs):
        out[...] = total[lax.rem(lax.axis_index("tensor") + s, parts)]


def pair_kernel(keep, came, *outs):
    for k, out in enumerate(outs):
        out[...] = (keep[k].astype(f32) + came[k].astype(f32)).astype(out.dtype)


def soap_kernel(old, basis, first_moment, second_rot, second_plain, *refs):
    parts, (slab_out, new_first, new_second, new_plain) = refs[:-4], refs[-4:]
    rows, heads, latent_dim = first_moment.shape
    flat = (heads * rows, latent_dim)

    def by_head(x):
        return jnp.swapaxes(x, 0, 1).reshape(flat)

    def by_row(x):
        return jnp.swapaxes(x.reshape(heads, rows, latent_dim), 0, 1)

    turn = basis[...].astype(bf16)
    grad = functools.reduce(jnp.add, [p[...].astype(f32) for p in parts]).reshape(flat)
    rotated = mm(grad.astype(bf16), turn)
    moment = beta_first * by_head(first_moment[...]) + (1.0 - beta_first) * rotated
    rot_sq = beta_second * by_head(second_rot[...]) + (1.0 - beta_second) * rotated * rotated
    plain_sq = beta_second * by_head(second_plain[...]) + (1.0 - beta_second) * grad * grad
    stacked = jnp.concatenate([moment / (jnp.sqrt(rot_sq) + epsilon), moment], axis=0).astype(bf16)
    turned = mm_nt(stacked, turn)
    direction = blend_share * turned[: flat[0]] + blend_share * turned[flat[0] :] / (jnp.sqrt(plain_sq) + epsilon)
    before = old[...].astype(f32)
    slab_out[...] = (before - learn_rate * (by_row(direction) + decay_rate * before)).astype(bf16)
    new_first[...] = by_row(moment)
    new_second[...] = by_row(rot_sq)
    new_plain[...] = by_row(plain_sq)


def row_copies(slabs, out, sems, core):
    chips, rows = len(slabs), slabs[0].shape[0]
    copies = []
    for k, slab in enumerate(slabs):
        chip = sender_chip(place_of()[0], k, chips)
        copies.append(pltpu.make_async_copy(slab, out.at[pl.ds((2 * chip + core) * rows, rows)], sems.at[k]))
    for copy in copies:
        copy.start()
    return copies


def place_own_kernel(chips, *refs):
    slabs, state, (out, *new_state, sems) = refs[:chips], refs[chips : chips + 3], refs[chips + 3 :]
    copies = row_copies(slabs, out, sems, place_of()[1])
    more = [pltpu.make_async_copy(a, b, sems.at[chips + i]) for i, (a, b) in enumerate(zip(state, new_state))]
    for copy in more:
        copy.start()
    for copy in copies + more:
        copy.wait()


def place_rest_kernel(chips, *refs):
    slabs, shares, (out, grad_latent, total, sems) = refs[1 : 1 + chips], refs[1 + chips : -4], refs[-4:]
    copies = row_copies(slabs, out, sems, 1 - place_of()[1])
    total[...] = functools.reduce(jnp.add, [x[...].astype(f32) for x in shares]).astype(bf16)
    last = pltpu.make_async_copy(total, grad_latent, sems.at[chips])
    last.start()
    for copy in copies + [last]:
        copy.wait()


def local(latent, q_nope, q_rope, k_rope, grad_out, offsets, weight, basis, first_moment, second_rot, second_plain):
    seq_len, latent_dim = latent.shape
    width, heads, _ = weight.shape
    dp, parts = lax.axis_size("dp"), lax.axis_size("tensor")
    chips = dp // 2
    rows = width // dp
    part_rows = seq_len // parts
    rope_dim = k_rope.shape[1]

    def core_swap(x):
        return lax.ppermute(x, "dp", [(i, i ^ 1) for i in range(dp)])

    def chip_move(x, k):
        if chips & (chips - 1):
            pairs = [(i, (i + 2 * k) % dp) for i in range(dp)]
        else:
            pairs = [(i, i ^ (2 * k)) for i in range(dp)]
        return lax.ppermute(x, "dp", pairs)

    def part_move(x, s):
        return lax.ppermute(x, "tensor", [(i, (i + s) % parts) for i in range(parts)])

    piece = (heads, rows, latent_dim)
    state = (rows, heads, latent_dim)
    send, keep, grad_kv, wall, own_weight = pl.pallas_call(
        attend_kernel,
        out_shape=(
            pltpu.VMEM((chips,) + piece, bf16),
            pltpu.VMEM((chips,) + piece, bf16),
            pltpu.VMEM((seq_len, heads * width), bf16),
            pltpu.VMEM((heads * width, latent_dim), bf16),
            pltpu.VMEM(state, bf16),
        ),
        in_specs=[in_vmem] + [in_hbm] * 6,
        out_specs=(in_vmem,) * 5,
        scratch_shapes=[
            pltpu.VMEM(latent.shape, bf16),
            pltpu.VMEM(q_nope.shape, bf16),
            pltpu.VMEM(q_rope.shape, bf16),
            pltpu.VMEM((rope_dim, seq_len), bf16),
            pltpu.VMEM(grad_out.shape, bf16),
            pltpu.VMEM(weight.shape, bf16),
            pltpu.VMEM((seq_len, heads * width), bf16),
            pltpu.VMEM((heads, dp, rows, latent_dim), f32),
            pltpu.SemaphoreType.DMA((6,)),
        ],
        compiler_params=limit_mib(32),
        cost_estimate=pl.CostEstimate(
            flops=12 * seq_len * heads * width * latent_dim, bytes_accessed=32 * 1024 * 1024, transcendentals=0
        ),
        name="attend",
    )(jnp.broadcast_to(offsets, (8, 128)), *[
        pltpu.with_memory_space_constraint(x, pltpu.HBM)
        for x in (
            latent, q_nope, q_rope, k_rope.T, grad_out, weight
        )
    ])

    send, basis, first_moment, second_rot, second_plain = lax.optimization_barrier(
        (send, basis, first_moment, second_rot, second_plain)
    )
    came = core_swap(send)
    glat = pl.pallas_call(
        latent_kernel,
        out_shape=[pltpu.VMEM((part_rows, latent_dim), bf16)] * parts,
        in_specs=[in_vmem] * 2,
        out_specs=[in_vmem] * parts,
        scratch_shapes=[pltpu.VMEM((parts, part_rows, latent_dim), bf16)],
        compiler_params=limit_mib(8),
        name="latent_share",
    )(grad_kv, wall)
    sums = pl.pallas_call(
        pair_kernel,
        out_shape=[pltpu.VMEM(piece, f32 if k == 0 else bf16) for k in range(chips)],
        in_specs=[in_vmem] * 2,
        out_specs=[in_vmem] * chips,
        compiler_params=limit_mib(4),
        name="pair_sum",
    )(keep, came)
    sums, glat = lax.optimization_barrier((sums, glat))
    got = [sums[0]] + [chip_move(sums[k], k) for k in range(1, chips)]
    glat = [glat[0]] + [part_move(glat[s], s) for s in range(1, parts)]

    new_slab, new_first, new_second, new_plain = pl.pallas_call(
        soap_kernel,
        out_shape=(pltpu.VMEM(state, bf16),) + (pltpu.VMEM(state, f32),) * 3,
        in_specs=[in_vmem] * (5 + chips),
        out_specs=(in_vmem,) * 4,
        compiler_params=limit_mib(8),
        name="soap",
    )(own_weight, basis, first_moment, second_rot, second_plain, *got)

    mine = [new_slab] + [chip_move(new_slab, k) for k in range(1, chips)]
    others = [core_swap(x) for x in mine]
    new_weight, new_first, new_second, new_plain = pl.pallas_call(
        functools.partial(place_own_kernel, chips),
        out_shape=(pltpu.HBM((width, heads, latent_dim), bf16),) + (pltpu.HBM(state, f32),) * 3,
        in_specs=[in_vmem] * (chips + 3),
        out_specs=(in_hbm,) * 4,
        scratch_shapes=[pltpu.SemaphoreType.DMA((chips + 3,))],
        compiler_params=limit_mib(4),
        name="place_own",
    )(*mine, new_first, new_second, new_plain)
    new_weight, grad_latent = pl.pallas_call(
        functools.partial(place_rest_kernel, chips),
        out_shape=(pltpu.HBM((width, heads, latent_dim), bf16), pltpu.HBM((part_rows, latent_dim), bf16)),
        in_specs=[in_hbm] + [in_vmem] * (chips + parts),
        out_specs=(in_hbm, in_hbm),
        scratch_shapes=[pltpu.VMEM((part_rows, latent_dim), bf16), pltpu.SemaphoreType.DMA((chips + 1,))],
        input_output_aliases={0: 0},
        compiler_params=limit_mib(4),
        name="place_rest",
    )(new_weight, *others, *glat)
    return (grad_latent, new_weight, new_first, new_second, new_plain)


def solution(mesh):
    state = P("dp", "tensor", None)
    return jax.shard_map(
        local,
        mesh=mesh,
        in_specs=(
            P("dp", None),
            P("dp", "tensor"),
            P("dp", "tensor"),
            P("dp", None),
            P("dp", "tensor"),
            P("dp"),
            P(None, "tensor", None),
            P(),
            state,
            state,
            state,
        ),
        out_specs=(P(("dp", "tensor"), None), P(None, "tensor", None), state, state, state),
        check_vma=False,
    )
```

```python
import functools

import jax
import jax.numpy as jnp
from jax import lax
from jax.experimental import pallas as pl
from jax.experimental.pallas import tpu as pltpu
from jax.sharding import PartitionSpec as P

beta_first = 0.9
beta_second = 0.95
epsilon = 1e-08
learn_rate = 0.002
decay_rate = 0.1
blend_share = 0.5
log2_e = 1.4426950408889634
f32 = jnp.float32
bf16 = jnp.bfloat16
in_vmem = pl.BlockSpec(memory_space=pltpu.VMEM)
in_hbm = pl.BlockSpec(memory_space=pltpu.HBM)


def mm(a, b):
    return lax.dot_general(a, b, (((1,), (0,)), ((), ())), preferred_element_type=f32)


def mm_nt(a, b):
    return lax.dot_general(a, b, (((1,), (1,)), ((), ())), preferred_element_type=f32)


def mm_tn(a, b):
    return lax.dot_general(a, b, (((0,), (0,)), ((), ())), preferred_element_type=f32)


def limit_mib(mib):
    return pltpu.CompilerParams(vmem_limit_bytes=mib * 1024 * 1024)


def other_chip(chip, k, chips):
    return lax.rem(chip + k, chips) if chips & (chips - 1) else chip ^ k


def sender_chip(chip, k, chips):
    return lax.rem(chip - k + chips, chips) if chips & (chips - 1) else chip ^ k


def place_of():
    me = lax.axis_index("dp")
    return lax.div(me, 2), lax.rem(me, 2)


def attend_kernel(
    offsets,
    latent,
    q_nope,
    q_rope,
    k_rope_t,
    grad_out,
    weight,
    send,
    keep,
    grad_kv,
    wall,
    own_weight,
    lat,
    q_main_v,
    q_side_v,
    k_side_v,
    g_out_v,
    weight_v,
    key_value,
    bias,
    slab,
    sems,
):
    seq_len, latent_dim = latent.shape
    width, heads, _ = weight.shape
    head_dim = width // 2
    rope_dim = k_rope_t.shape[0]
    chips, _, rows, _ = keep.shape
    scale = float(head_dim + rope_dim) ** (-0.5)
    pairs = [
        (weight, weight_v),
        (latent, lat),
        (k_rope_t, k_side_v),
        (q_nope, q_main_v),
        (q_rope, q_side_v),
        (grad_out, g_out_v),
    ]
    copies = [pltpu.make_async_copy(a, b, sems.at[i]) for i, (a, b) in enumerate(pairs)]
    for copy in copies[:2]:
        copy.start()
    limit = jnp.maximum(lax.broadcasted_iota(jnp.int32, (1, seq_len), 1), offsets[:1, :1] - 1)
    bias[...] = jnp.where(lax.broadcasted_iota(jnp.int32, (seq_len, seq_len), 0) <= limit, 0.0, -1e30)
    zeros = jnp.zeros((seq_len, head_dim), bf16)
    for copy in copies[2:]:
        copy.start(priority=1)
    copies[0].wait()
    wall[...] = jnp.swapaxes(weight_v[...], 0, 1).reshape(heads * width, latent_dim)
    copies[1].wait()
    key_value[...] = mm_nt(lat[...], wall[...]).astype(bf16)
    for copy in copies[2:6]:
        copy.wait()
    k_side = k_side_v[...].T
    for h in range(heads):
        q_main = q_main_v[:, h * head_dim : (h + 1) * head_dim]
        g_out = g_out_v[:, h * head_dim : (h + 1) * head_dim]
        q_all = jnp.concatenate([q_main, q_side_v[:, h * rope_dim : (h + 1) * rope_dim]], axis=1)
        keys = key_value[:, h * width : h * width + head_dim]
        values = key_value[:, h * width + head_dim : (h + 1) * width]
        k_all = jnp.concatenate([keys, k_side], axis=1)
        scores = mm_nt(k_all, q_all) + bias[...]
        top = jnp.max(scores, axis=0, keepdims=True)
        terms = jnp.exp2((scores - top) * (scale * log2_e))
        inv = 1.0 / jnp.sum(terms, axis=0, keepdims=True)
        probs = terms * inv
        probs_low = probs.astype(bf16)
        grad_probs = mm_nt(values, g_out)
        delta = jnp.sum(probs * grad_probs, axis=0, keepdims=True)
        grad_scores = (probs * (grad_probs - delta) * scale).astype(bf16)
        lhs = jnp.concatenate([grad_scores, zeros[:, : -seq_len % 128], probs_low], axis=1)
        rhs = jnp.concatenate(
            [
                jnp.concatenate([q_main, zeros], axis=1),
                jnp.concatenate([zeros, zeros], axis=1)[: -seq_len % 128],
                jnp.concatenate([zeros, g_out], axis=1),
            ],
            axis=0,
        )
        grad_kv[:, h * width : (h + 1) * width] = mm(lhs, rhs).astype(bf16)
    slab[...] = mm_tn(grad_kv[...], lat[...]).reshape(heads, 2 * chips, rows, latent_dim)
    my_chip, my_core = place_of()
    for k in range(chips):
        chip = other_chip(my_chip, k, chips)
        for h in range(heads):
            send[k, h] = slab[h, 2 * chip + 1 - my_core].astype(bf16)
            keep[k, h] = slab[h, 2 * chip + my_core].astype(bf16)
    own_weight[...] = weight_v[pl.ds((2 * my_chip + my_core) * rows, rows)]


def latent_kernel(grad_kv, wall, *refs):
    total, outs = refs[-1], refs[:-1]
    parts = len(outs)
    total[...] = mm(grad_kv[...], wall[...]).astype(bf16).reshape(total.shape)
    for s, out in enumerate(outs):
        out[...] = total[lax.rem(lax.axis_index("tensor") + s, parts)]


def pair_kernel(keep, came, *outs):
    for k, out in enumerate(outs):
        out[...] = (keep[k].astype(f32) + came[k].astype(f32)).astype(out.dtype)


def by_head(x):
    return jnp.swapaxes(x, 0, 1).reshape(x.shape[0] * x.shape[1], x.shape[2])


def ready_kernel(old, basis, first_moment, second_rot, second_plain, before, turn, first, rot, plain):
    before[...] = by_head(old[...].astype(f32))
    turn[...] = basis[...].astype(bf16)
    first[...] = by_head(beta_first * first_moment[...])
    rot[...] = by_head(beta_second * second_rot[...])
    plain[...] = by_head(beta_second * second_plain[...])


def soap_kernel(before, turn, first, rot, plain, *refs):
    parts, (slab_out, new_first, new_second, new_plain) = refs[:-4], refs[-4:]
    rows, heads, latent_dim = new_first.shape
    count = rows * heads

    def by_row(x):
        return jnp.swapaxes(x.reshape(heads, rows, latent_dim), 0, 1)

    grad = functools.reduce(jnp.add, [p[...].astype(f32) for p in parts]).reshape(count, latent_dim)
    rotated = mm(grad.astype(bf16), turn[...])
    moment = first[...] + (1.0 - beta_first) * rotated
    rot_sq = rot[...] + (1.0 - beta_second) * rotated * rotated
    plain_sq = plain[...] + (1.0 - beta_second) * grad * grad
    stacked = jnp.concatenate([moment / (jnp.sqrt(rot_sq) + epsilon), moment], axis=0).astype(bf16)
    turned = mm_nt(stacked, turn[...])
    direction = blend_share * turned[:count] + blend_share * turned[count:] / (jnp.sqrt(plain_sq) + epsilon)
    old = before[...]
    slab_out[...] = by_row(old - learn_rate * (direction + decay_rate * old)).astype(bf16)
    new_first[...] = by_row(moment)
    new_second[...] = by_row(rot_sq)
    new_plain[...] = by_row(plain_sq)


def row_copies(slabs, out, sems, core):
    chips, rows = len(slabs), slabs[0].shape[0]
    copies = []
    for k, slab in enumerate(slabs):
        chip = sender_chip(place_of()[0], k, chips)
        copies.append(pltpu.make_async_copy(slab, out.at[pl.ds((2 * chip + core) * rows, rows)], sems.at[k]))
    for copy in copies:
        copy.start()
    return copies


def place_own_kernel(chips, *refs):
    slabs, state, (out, *new_state, sems) = refs[:chips], refs[chips : chips + 3], refs[chips + 3 :]
    copies = row_copies(slabs, out, sems, place_of()[1])
    more = [pltpu.make_async_copy(a, b, sems.at[chips + i]) for i, (a, b) in enumerate(zip(state, new_state))]
    for copy in more:
        copy.start()
    for copy in copies + more:
        copy.wait()


def place_rest_kernel(chips, *refs):
    slabs, shares, (out, grad_latent, total, sems) = refs[1 : 1 + chips], refs[1 + chips : -4], refs[-4:]
    copies = row_copies(slabs, out, sems, 1 - place_of()[1])
    total[...] = functools.reduce(jnp.add, [x[...].astype(f32) for x in shares]).astype(bf16)
    last = pltpu.make_async_copy(total, grad_latent, sems.at[chips])
    last.start()
    for copy in copies + [last]:
        copy.wait()


def local(latent, q_nope, q_rope, k_rope, grad_out, offsets, weight, basis, first_moment, second_rot, second_plain):
    seq_len, latent_dim = latent.shape
    width, heads, _ = weight.shape
    dp, parts = lax.axis_size("dp"), lax.axis_size("tensor")
    chips = dp // 2
    rows = width // dp
    part_rows = seq_len // parts
    rope_dim = k_rope.shape[1]

    def core_swap(x):
        return lax.ppermute(x, "dp", [(i, i ^ 1) for i in range(dp)])

    def chip_move(x, k):
        if chips & (chips - 1):
            pairs = [(i, (i + 2 * k) % dp) for i in range(dp)]
        else:
            pairs = [(i, i ^ (2 * k)) for i in range(dp)]
        return lax.ppermute(x, "dp", pairs)

    def part_move(x, s):
        return lax.ppermute(x, "tensor", [(i, (i + s) % parts) for i in range(parts)])

    piece = (heads, rows, latent_dim)
    state = (rows, heads, latent_dim)
    send, keep, grad_kv, wall, own_weight = pl.pallas_call(
        attend_kernel,
        out_shape=(
            pltpu.VMEM((chips,) + piece, bf16),
            pltpu.VMEM((chips,) + piece, bf16),
            pltpu.VMEM((seq_len, heads * width), bf16),
            pltpu.VMEM((heads * width, latent_dim), bf16),
            pltpu.VMEM(state, bf16),
        ),
        in_specs=[in_vmem] + [in_hbm] * 6,
        out_specs=(in_vmem,) * 5,
        scratch_shapes=[
            pltpu.VMEM(latent.shape, bf16),
            pltpu.VMEM(q_nope.shape, bf16),
            pltpu.VMEM(q_rope.shape, bf16),
            pltpu.VMEM((rope_dim, seq_len), bf16),
            pltpu.VMEM(grad_out.shape, bf16),
            pltpu.VMEM(weight.shape, bf16),
            pltpu.VMEM((seq_len, heads * width), bf16),
            pltpu.VMEM((seq_len, seq_len), f32),
            pltpu.VMEM((heads, dp, rows, latent_dim), f32),
            pltpu.SemaphoreType.DMA((6,)),
        ],
        compiler_params=limit_mib(32),
        cost_estimate=pl.CostEstimate(
            flops=12 * seq_len * heads * width * latent_dim, bytes_accessed=32 * 1024 * 1024, transcendentals=0
        ),
        name="attend",
    )(jnp.broadcast_to(offsets, (8, 128)), *[
        pltpu.with_memory_space_constraint(x, pltpu.HBM)
        for x in (
            latent, q_nope, q_rope, k_rope.T, grad_out, weight
        )
    ])

    send, basis, first_moment, second_rot, second_plain = lax.optimization_barrier(
        (send, basis, first_moment, second_rot, second_plain)
    )
    came = core_swap(send)
    glat = pl.pallas_call(
        latent_kernel,
        out_shape=[pltpu.VMEM((part_rows, latent_dim), bf16)] * parts,
        in_specs=[in_vmem] * 2,
        out_specs=[in_vmem] * parts,
        scratch_shapes=[pltpu.VMEM((parts, part_rows, latent_dim), bf16)],
        compiler_params=limit_mib(8),
        name="latent_share",
    )(grad_kv, wall)
    sums = pl.pallas_call(
        pair_kernel,
        out_shape=[pltpu.VMEM(piece, f32 if k == 0 else bf16) for k in range(chips)],
        in_specs=[in_vmem] * 2,
        out_specs=[in_vmem] * chips,
        compiler_params=limit_mib(4),
        name="pair_sum",
    )(keep, came)
    sums, glat = lax.optimization_barrier((sums, glat))
    got = [sums[0]] + [chip_move(sums[k], k) for k in range(1, chips)]
    glat = [glat[0]] + [part_move(glat[s], s) for s in range(1, parts)]

    flat = (heads * rows, latent_dim)
    ready = pl.pallas_call(
        ready_kernel,
        out_shape=[pltpu.VMEM(flat, f32), pltpu.VMEM(basis.shape, bf16)] + [pltpu.VMEM(flat, f32)] * 3,
        in_specs=[in_vmem] * 5,
        out_specs=[in_vmem] * 5,
        compiler_params=limit_mib(8),
        name="ready",
    )(own_weight, basis, first_moment, second_rot, second_plain)
    new_slab, new_first, new_second, new_plain = pl.pallas_call(
        soap_kernel,
        out_shape=(pltpu.VMEM(state, bf16),) + (pltpu.VMEM(state, f32),) * 3,
        in_specs=[in_vmem] * (5 + chips),
        out_specs=(in_vmem,) * 4,
        compiler_params=limit_mib(8),
        name="soap",
    )(*ready, *got)

    mine = [new_slab] + [chip_move(new_slab, k) for k in range(1, chips)]
    others = [core_swap(x) for x in mine]
    new_weight, new_first, new_second, new_plain = pl.pallas_call(
        functools.partial(place_own_kernel, chips),
        out_shape=(pltpu.HBM((width, heads, latent_dim), bf16),) + (pltpu.HBM(state, f32),) * 3,
        in_specs=[in_vmem] * (chips + 3),
        out_specs=(in_hbm,) * 4,
        scratch_shapes=[pltpu.SemaphoreType.DMA((chips + 3,))],
        compiler_params=limit_mib(4),
        name="place_own",
    )(*mine, new_first, new_second, new_plain)
    new_weight, grad_latent = pl.pallas_call(
        functools.partial(place_rest_kernel, chips),
        out_shape=(pltpu.HBM((width, heads, latent_dim), bf16), pltpu.HBM((part_rows, latent_dim), bf16)),
        in_specs=[in_hbm] + [in_vmem] * (chips + parts),
        out_specs=(in_hbm, in_hbm),
        scratch_shapes=[pltpu.VMEM((part_rows, latent_dim), bf16), pltpu.SemaphoreType.DMA((chips + 1,))],
        input_output_aliases={0: 0},
        compiler_params=limit_mib(4),
        name="place_rest",
    )(new_weight, *others, *glat)
    return (grad_latent, new_weight, new_first, new_second, new_plain)


def solution(mesh):
    state = P("dp", "tensor", None)
    return jax.shard_map(
        local,
        mesh=mesh,
        in_specs=(
            P("dp", None),
            P("dp", "tensor"),
            P("dp", "tensor"),
            P("dp", None),
            P("dp", "tensor"),
            P("dp"),
            P(None, "tensor", None),
            P(),
            state,
            state,
            state,
        ),
        out_specs=(P(("dp", "tensor"), None), P(None, "tensor", None), state, state, state),
        check_vma=False,
    )
```

```python
import functools

import jax
import jax.numpy as jnp
from jax import lax
from jax.experimental import pallas as pl
from jax.experimental.pallas import tpu as pltpu
from jax.sharding import PartitionSpec as P

beta_first = 0.9
beta_second = 0.95
epsilon = 1e-08
learn_rate = 0.002
decay_rate = 0.1
blend_share = 0.5
log2_e = 1.4426950408889634
f32 = jnp.float32
bf16 = jnp.bfloat16
in_vmem = pl.BlockSpec(memory_space=pltpu.VMEM)
in_hbm = pl.BlockSpec(memory_space=pltpu.HBM)


def mm(a, b):
    return lax.dot_general(a, b, (((1,), (0,)), ((), ())), preferred_element_type=f32)


def mm_nt(a, b):
    return lax.dot_general(a, b, (((1,), (1,)), ((), ())), preferred_element_type=f32)


def mm_tn(a, b):
    return lax.dot_general(a, b, (((0,), (0,)), ((), ())), preferred_element_type=f32)


def limit_mib(mib):
    return pltpu.CompilerParams(vmem_limit_bytes=mib * 1024 * 1024)


def other_chip(chip, k, chips):
    return lax.rem(chip + k, chips) if chips & (chips - 1) else chip ^ k


def sender_chip(chip, k, chips):
    return lax.rem(chip - k + chips, chips) if chips & (chips - 1) else chip ^ k


def place_of():
    me = lax.axis_index("dp")
    return lax.div(me, 2), lax.rem(me, 2)


def attend_kernel(
    offsets,
    latent,
    q_nope,
    q_rope,
    k_rope_t,
    grad_out,
    weight,
    send,
    keep,
    grad_kv,
    wall,
    own_weight,
    lat,
    q_main_v,
    q_side_v,
    k_side_v,
    g_out_v,
    weight_v,
    bias,
    slab,
    sems,
):
    seq_len, latent_dim = latent.shape
    width, heads, _ = weight.shape
    head_dim = width // 2
    rope_dim = k_rope_t.shape[0]
    chips, _, rows, _ = keep.shape
    scale = float(head_dim + rope_dim) ** (-0.5)
    pairs = [
        (weight, weight_v),
        (latent, lat),
        (k_rope_t, k_side_v),
        (q_nope, q_main_v),
        (q_rope, q_side_v),
        (grad_out, g_out_v),
    ]
    copies = [pltpu.make_async_copy(a, b, sems.at[i]) for i, (a, b) in enumerate(pairs)]
    for copy in copies[:2]:
        copy.start()
    limit = jnp.maximum(lax.broadcasted_iota(jnp.int32, (1, seq_len), 1), offsets[:1, :1] - 1)
    bias[...] = jnp.where(lax.broadcasted_iota(jnp.int32, (seq_len, seq_len), 0) <= limit, 0.0, -1e30)
    zeros = jnp.zeros((seq_len, head_dim), bf16)
    for copy in copies[2:]:
        copy.start(priority=1)
    copies[0].wait()
    wall[...] = jnp.swapaxes(weight_v[...], 0, 1).reshape(heads * width, latent_dim)
    copies[1].wait()
    kv_all = mm_nt(lat[...], wall[...]).astype(bf16)
    for copy in copies[2:6]:
        copy.wait()
    k_side = k_side_v[...].T
    found = []
    for h in range(heads):
        q_main = q_main_v[:, h * head_dim : (h + 1) * head_dim]
        g_out = g_out_v[:, h * head_dim : (h + 1) * head_dim]
        q_all = jnp.concatenate([q_main, q_side_v[:, h * rope_dim : (h + 1) * rope_dim]], axis=1)
        keys = kv_all[:, h * width : h * width + head_dim]
        values = kv_all[:, h * width + head_dim : (h + 1) * width]
        k_all = jnp.concatenate([keys, k_side], axis=1)
        scores = mm_nt(k_all, q_all) + bias[...]
        top = jnp.max(scores, axis=0, keepdims=True)
        terms = jnp.exp2((scores - top) * (scale * log2_e))
        inv = 1.0 / jnp.sum(terms, axis=0, keepdims=True)
        probs = terms * inv
        probs_low = probs.astype(bf16)
        grad_probs = mm_nt(values, g_out)
        delta = jnp.sum(probs * grad_probs, axis=0, keepdims=True)
        grad_scores = (probs * (grad_probs - delta)).astype(bf16)
        lhs = jnp.concatenate([grad_scores, zeros[:, : -seq_len % 128], probs_low], axis=1)
        rhs = jnp.concatenate(
            [
                jnp.concatenate([q_main, zeros], axis=1),
                jnp.concatenate([zeros, zeros], axis=1)[: -seq_len % 128],
                jnp.concatenate([zeros, g_out], axis=1),
            ],
            axis=0,
        )
        pair = mm(lhs, rhs)
        found.append(jnp.concatenate([pair[:, :head_dim] * scale, pair[:, head_dim:]], axis=1).astype(bf16))
    found = jnp.concatenate(found, axis=1)
    grad_kv[...] = found
    slab[...] = mm_tn(found, lat[...]).reshape(heads, 2 * chips, rows, latent_dim).astype(bf16)
    my_chip, my_core = place_of()
    for k in range(chips):
        chip = other_chip(my_chip, k, chips)
        for h in range(heads):
            send[k, h] = slab[h, 2 * chip + 1 - my_core]
            keep[k, h] = slab[h, 2 * chip + my_core]
    own_weight[...] = weight_v[pl.ds((2 * my_chip + my_core) * rows, rows)]


def latent_kernel(grad_kv, wall, *refs):
    total, outs = refs[-1], refs[:-1]
    parts = len(outs)
    total[...] = mm(grad_kv[...], wall[...]).astype(bf16).reshape(total.shape)
    for s, out in enumerate(outs):
        out[...] = total[lax.rem(lax.axis_index("tensor") + s, parts)]


def pair_kernel(keep, came, *outs):
    for k, out in enumerate(outs):
        out[...] = (keep[k].astype(f32) + came[k].astype(f32)).astype(out.dtype)


def by_head(x):
    return jnp.swapaxes(x, 0, 1).reshape(x.shape[0] * x.shape[1], x.shape[2])


def ready_kernel(old, basis, first_moment, second_rot, second_plain, before, turn, first, rot, plain):
    before[...] = by_head(old[...].astype(f32))
    turn[...] = basis[...].astype(bf16)
    first[...] = by_head(beta_first * first_moment[...])
    rot[...] = by_head(beta_second * second_rot[...])
    plain[...] = by_head(beta_second * second_plain[...])


def soap_kernel(before, turn, first, rot, plain, *refs):
    parts, (slab_out, new_first, new_second, new_plain) = refs[:-4], refs[-4:]
    rows, heads, latent_dim = new_first.shape
    count = rows * heads

    def by_row(x):
        return jnp.swapaxes(x.reshape(heads, rows, latent_dim), 0, 1)

    grad = functools.reduce(jnp.add, [p[...].astype(f32) for p in parts]).reshape(count, latent_dim)
    rotated = mm(grad.astype(bf16), turn[...])
    moment = first[...] + (1.0 - beta_first) * rotated
    rot_sq = rot[...] + (1.0 - beta_second) * rotated * rotated
    plain_sq = plain[...] + (1.0 - beta_second) * grad * grad
    stacked = jnp.concatenate([moment / (jnp.sqrt(rot_sq) + epsilon), moment], axis=0).astype(bf16)
    turned = mm_nt(stacked, turn[...])
    direction = blend_share * turned[:count] + blend_share * turned[count:] / (jnp.sqrt(plain_sq) + epsilon)
    old = before[...]
    slab_out[...] = by_row(old - learn_rate * (direction + decay_rate * old)).astype(bf16)
    new_first[...] = by_row(moment)
    new_second[...] = by_row(rot_sq)
    new_plain[...] = by_row(plain_sq)


def row_copies(slabs, out, sems, core):
    chips, rows = len(slabs), slabs[0].shape[0]
    copies = []
    for k, slab in enumerate(slabs):
        chip = sender_chip(place_of()[0], k, chips)
        copies.append(pltpu.make_async_copy(slab, out.at[pl.ds((2 * chip + core) * rows, rows)], sems.at[k]))
    for copy in copies:
        copy.start()
    return copies


def place_own_kernel(chips, *refs):
    slabs, state, (out, *new_state, sems) = refs[:chips], refs[chips : chips + 3], refs[chips + 3 :]
    copies = row_copies(slabs, out, sems, place_of()[1])
    more = [pltpu.make_async_copy(a, b, sems.at[chips + i]) for i, (a, b) in enumerate(zip(state, new_state))]
    for copy in more:
        copy.start()
    for copy in copies + more:
        copy.wait()


def place_rest_kernel(chips, *refs):
    slabs, shares, (out, grad_latent, total, sems) = refs[1 : 1 + chips], refs[1 + chips : -4], refs[-4:]
    copies = row_copies(slabs, out, sems, 1 - place_of()[1])
    total[...] = functools.reduce(jnp.add, [x[...].astype(f32) for x in shares]).astype(bf16)
    last = pltpu.make_async_copy(total, grad_latent, sems.at[chips])
    last.start()
    for copy in copies + [last]:
        copy.wait()


def local(latent, q_nope, q_rope, k_rope, grad_out, offsets, weight, basis, first_moment, second_rot, second_plain):
    seq_len, latent_dim = latent.shape
    width, heads, _ = weight.shape
    dp, parts = lax.axis_size("dp"), lax.axis_size("tensor")
    chips = dp // 2
    rows = width // dp
    part_rows = seq_len // parts
    rope_dim = k_rope.shape[1]

    def core_swap(x):
        return lax.ppermute(x, "dp", [(i, i ^ 1) for i in range(dp)])

    def chip_move(x, k):
        if chips & (chips - 1):
            pairs = [(i, (i + 2 * k) % dp) for i in range(dp)]
        else:
            pairs = [(i, i ^ (2 * k)) for i in range(dp)]
        return lax.ppermute(x, "dp", pairs)

    def part_move(x, s):
        return lax.ppermute(x, "tensor", [(i, (i + s) % parts) for i in range(parts)])

    piece = (heads, rows, latent_dim)
    state = (rows, heads, latent_dim)
    send, keep, grad_kv, wall, own_weight = pl.pallas_call(
        attend_kernel,
        out_shape=(
            pltpu.VMEM((chips,) + piece, bf16),
            pltpu.VMEM((chips,) + piece, bf16),
            pltpu.VMEM((seq_len, heads * width), bf16),
            pltpu.VMEM((heads * width, latent_dim), bf16),
            pltpu.VMEM(state, bf16),
        ),
        in_specs=[in_vmem] + [in_hbm] * 6,
        out_specs=(in_vmem,) * 5,
        scratch_shapes=[
            pltpu.VMEM(latent.shape, bf16),
            pltpu.VMEM(q_nope.shape, bf16),
            pltpu.VMEM(q_rope.shape, bf16),
            pltpu.VMEM((rope_dim, seq_len), bf16),
            pltpu.VMEM(grad_out.shape, bf16),
            pltpu.VMEM(weight.shape, bf16),
            pltpu.VMEM((seq_len, seq_len), f32),
            pltpu.VMEM((heads, dp, rows, latent_dim), bf16),
            pltpu.SemaphoreType.DMA((6,)),
        ],
        compiler_params=limit_mib(32),
        cost_estimate=pl.CostEstimate(
            flops=12 * seq_len * heads * width * latent_dim, bytes_accessed=32 * 1024 * 1024, transcendentals=0
        ),
        name="attend",
    )(jnp.broadcast_to(offsets, (8, 128)), *[
        pltpu.with_memory_space_constraint(x, pltpu.HBM)
        for x in (
            latent, q_nope, q_rope, k_rope.T, grad_out, weight
        )
    ])

    send, basis, first_moment, second_rot, second_plain = lax.optimization_barrier(
        (send, basis, first_moment, second_rot, second_plain)
    )
    came = core_swap(send)
    glat = pl.pallas_call(
        latent_kernel,
        out_shape=[pltpu.VMEM((part_rows, latent_dim), bf16)] * parts,
        in_specs=[in_vmem] * 2,
        out_specs=[in_vmem] * parts,
        scratch_shapes=[pltpu.VMEM((parts, part_rows, latent_dim), bf16)],
        compiler_params=limit_mib(8),
        name="latent_share",
    )(grad_kv, wall)
    sums = pl.pallas_call(
        pair_kernel,
        out_shape=[pltpu.VMEM(piece, f32 if k == 0 else bf16) for k in range(chips)],
        in_specs=[in_vmem] * 2,
        out_specs=[in_vmem] * chips,
        compiler_params=limit_mib(4),
        name="pair_sum",
    )(keep, came)
    sums, glat = lax.optimization_barrier((sums, glat))
    got = [sums[0]] + [chip_move(sums[k], k) for k in range(1, chips)]
    glat = [glat[0]] + [part_move(glat[s], s) for s in range(1, parts)]

    flat = (heads * rows, latent_dim)
    ready = pl.pallas_call(
        ready_kernel,
        out_shape=[pltpu.VMEM(flat, f32), pltpu.VMEM(basis.shape, bf16)] + [pltpu.VMEM(flat, f32)] * 3,
        in_specs=[in_vmem] * 5,
        out_specs=[in_vmem] * 5,
        compiler_params=limit_mib(8),
        name="ready",
    )(own_weight, basis, first_moment, second_rot, second_plain)
    new_slab, new_first, new_second, new_plain = pl.pallas_call(
        soap_kernel,
        out_shape=(pltpu.VMEM(state, bf16),) + (pltpu.VMEM(state, f32),) * 3,
        in_specs=[in_vmem] * (5 + chips),
        out_specs=(in_vmem,) * 4,
        compiler_params=limit_mib(8),
        name="soap",
    )(*ready, *got)

    mine = [new_slab] + [chip_move(new_slab, k) for k in range(1, chips)]
    others = [core_swap(x) for x in mine]
    new_weight, new_first, new_second, new_plain = pl.pallas_call(
        functools.partial(place_own_kernel, chips),
        out_shape=(pltpu.HBM((width, heads, latent_dim), bf16),) + (pltpu.HBM(state, f32),) * 3,
        in_specs=[in_vmem] * (chips + 3),
        out_specs=(in_hbm,) * 4,
        scratch_shapes=[pltpu.SemaphoreType.DMA((chips + 3,))],
        compiler_params=limit_mib(4),
        name="place_own",
    )(*mine, new_first, new_second, new_plain)
    new_weight, grad_latent = pl.pallas_call(
        functools.partial(place_rest_kernel, chips),
        out_shape=(pltpu.HBM((width, heads, latent_dim), bf16), pltpu.HBM((part_rows, latent_dim), bf16)),
        in_specs=[in_hbm] + [in_vmem] * (chips + parts),
        out_specs=(in_hbm, in_hbm),
        scratch_shapes=[pltpu.VMEM((part_rows, latent_dim), bf16), pltpu.SemaphoreType.DMA((chips + 1,))],
        input_output_aliases={0: 0},
        compiler_params=limit_mib(4),
        name="place_rest",
    )(new_weight, *others, *glat)
    return (grad_latent, new_weight, new_first, new_second, new_plain)


def solution(mesh):
    state = P("dp", "tensor", None)
    return jax.shard_map(
        local,
        mesh=mesh,
        in_specs=(
            P("dp", None),
            P("dp", "tensor"),
            P("dp", "tensor"),
            P("dp", None),
            P("dp", "tensor"),
            P("dp"),
            P(None, "tensor", None),
            P(),
            state,
            state,
            state,
        ),
        out_specs=(P(("dp", "tensor"), None), P(None, "tensor", None), state, state, state),
        check_vma=False,
    )
```

```python
import functools

import jax
import jax.numpy as jnp
from jax import lax
from jax.experimental import pallas as pl
from jax.experimental.pallas import tpu as pltpu
from jax.sharding import PartitionSpec as P

beta_first = 0.9
beta_second = 0.95
epsilon = 1e-08
learn_rate = 0.002
decay_rate = 0.1
blend_share = 0.5
log2_e = 1.4426950408889634
f32 = jnp.float32
bf16 = jnp.bfloat16
in_vmem = pl.BlockSpec(memory_space=pltpu.VMEM)
in_hbm = pl.BlockSpec(memory_space=pltpu.HBM)


def mm(a, b):
    return lax.dot_general(a, b, (((1,), (0,)), ((), ())), preferred_element_type=f32)


def mm_nt(a, b):
    return lax.dot_general(a, b, (((1,), (1,)), ((), ())), preferred_element_type=f32)


def mm_tn(a, b):
    return lax.dot_general(a, b, (((0,), (0,)), ((), ())), preferred_element_type=f32)


def limit_mib(mib):
    return pltpu.CompilerParams(vmem_limit_bytes=mib * 1024 * 1024)


def other_chip(chip, k, chips):
    return lax.rem(chip + k, chips) if chips & (chips - 1) else chip ^ k


def sender_chip(chip, k, chips):
    return lax.rem(chip - k + chips, chips) if chips & (chips - 1) else chip ^ k


def place_of():
    me = lax.axis_index("dp")
    return lax.div(me, 2), lax.rem(me, 2)


def attend_kernel(
    offsets,
    latent,
    q_nope,
    q_rope,
    k_rope_t,
    grad_out,
    weight,
    send,
    keep,
    grad_kv,
    wall,
    own_weight,
    lat,
    q_main_v,
    q_side_v,
    k_side_v,
    g_out_v,
    weight_v,
    bias,
    slab,
    sems,
):
    seq_len, latent_dim = latent.shape
    width, heads, _ = weight.shape
    head_dim = width // 2
    rope_dim = k_rope_t.shape[0]
    chips, _, rows, _ = keep.shape
    scale = float(head_dim + rope_dim) ** (-0.5)
    pairs = [
        (weight, weight_v),
        (latent, lat),
        (k_rope_t, k_side_v),
        (q_nope, q_main_v),
        (q_rope, q_side_v),
        (grad_out, g_out_v),
    ]
    copies = [pltpu.make_async_copy(a, b, sems.at[i]) for i, (a, b) in enumerate(pairs)]
    for copy in copies[:2]:
        copy.start()
    limit = jnp.maximum(lax.broadcasted_iota(jnp.int32, (1, seq_len), 1), offsets[:1, :1] - 1)
    bias[...] = jnp.where(lax.broadcasted_iota(jnp.int32, (seq_len, seq_len), 0) <= limit, 0.0, -1e30)
    zeros = jnp.zeros((seq_len, head_dim), bf16)
    for copy in copies[2:]:
        copy.start(priority=1)
    copies[0].wait()
    wall[...] = jnp.swapaxes(weight_v[...], 0, 1).reshape(heads * width, latent_dim)
    copies[1].wait()
    kv_all = mm_nt(lat[...], wall[...]).astype(bf16)
    for copy in copies[2:6]:
        copy.wait()
    k_side = k_side_v[...].T

    def masked(scores):
        blocks = []
        for lo in range(0, seq_len, 128):
            hi = min(lo + 128, seq_len)
            part = scores[lo:hi, :hi] + bias[lo:hi, :hi]
            blocks.append(jnp.concatenate([part, scores[lo:hi, hi:]], axis=1) if hi < seq_len else part)
        return jnp.concatenate(blocks, axis=0)

    found = []
    for h in range(heads):
        q_main = q_main_v[:, h * head_dim : (h + 1) * head_dim]
        g_out = g_out_v[:, h * head_dim : (h + 1) * head_dim]
        q_all = jnp.concatenate([q_main, q_side_v[:, h * rope_dim : (h + 1) * rope_dim]], axis=1)
        keys = kv_all[:, h * width : h * width + head_dim]
        values = kv_all[:, h * width + head_dim : (h + 1) * width]
        k_all = jnp.concatenate([keys, k_side], axis=1)
        scores = masked(mm_nt(k_all, q_all))
        top = jnp.max(scores, axis=0, keepdims=True)
        terms = jnp.exp2((scores - top) * (scale * log2_e))
        inv = 1.0 / jnp.sum(terms, axis=0, keepdims=True)
        probs = terms * inv
        probs_low = probs.astype(bf16)
        grad_probs = mm_nt(values, g_out)
        delta = jnp.sum(probs * grad_probs, axis=0, keepdims=True)
        grad_scores = (probs * (grad_probs - delta)).astype(bf16)
        lhs = jnp.concatenate([grad_scores, zeros[:, : -seq_len % 128], probs_low], axis=1)
        rhs = jnp.concatenate(
            [
                jnp.concatenate([q_main, zeros], axis=1),
                jnp.concatenate([zeros, zeros], axis=1)[: -seq_len % 128],
                jnp.concatenate([zeros, g_out], axis=1),
            ],
            axis=0,
        )
        pair = mm(lhs, rhs)
        found.append(jnp.concatenate([pair[:, :head_dim] * scale, pair[:, head_dim:]], axis=1).astype(bf16))
    found = jnp.concatenate(found, axis=1)
    grad_kv[...] = found
    slab[...] = mm_tn(found, lat[...]).reshape(heads, 2 * chips, rows, latent_dim).astype(bf16)
    my_chip, my_core = place_of()
    for k in range(chips):
        chip = other_chip(my_chip, k, chips)
        for h in range(heads):
            send[k, h] = slab[h, 2 * chip + 1 - my_core]
            keep[k, h] = slab[h, 2 * chip + my_core]
    own_weight[...] = weight_v[pl.ds((2 * my_chip + my_core) * rows, rows)]


def latent_kernel(grad_kv, wall, *refs):
    total, outs = refs[-1], refs[:-1]
    parts = len(outs)
    total[...] = mm(grad_kv[...], wall[...]).astype(bf16).reshape(total.shape)
    for s, out in enumerate(outs):
        out[...] = total[lax.rem(lax.axis_index("tensor") + s, parts)]


def pair_kernel(keep, came, *outs):
    for k, out in enumerate(outs):
        out[...] = (keep[k].astype(f32) + came[k].astype(f32)).astype(out.dtype)


def by_head(x):
    return jnp.swapaxes(x, 0, 1).reshape(x.shape[0] * x.shape[1], x.shape[2])


def ready_kernel(old, basis, first_moment, second_rot, second_plain, before, turn, first, rot, plain):
    before[...] = by_head(old[...].astype(f32))
    turn[...] = basis[...].astype(bf16)
    first[...] = by_head(beta_first * first_moment[...])
    rot[...] = by_head(beta_second * second_rot[...])
    plain[...] = by_head(beta_second * second_plain[...])


def by_row(x, heads):
    return jnp.swapaxes(x.reshape(heads, x.shape[0] // heads, x.shape[1]), 0, 1)


def soap_kernel(before, turn, first, rot, plain, *refs):
    parts, (slab_out, new_first, new_second, new_plain) = refs[:-4], refs[-4:]
    rows, heads, latent_dim = slab_out.shape
    count = rows * heads

    grad = functools.reduce(jnp.add, [p[...].astype(f32) for p in parts]).reshape(count, latent_dim)
    rotated = mm(grad.astype(bf16), turn[...])
    moment = first[...] + (1.0 - beta_first) * rotated
    rot_sq = rot[...] + (1.0 - beta_second) * rotated * rotated
    plain_sq = plain[...] + (1.0 - beta_second) * grad * grad
    stacked = jnp.concatenate([moment / (jnp.sqrt(rot_sq) + epsilon), moment], axis=0).astype(bf16)
    turned = mm_nt(stacked, turn[...])
    direction = blend_share * turned[:count] + blend_share * turned[count:] / (jnp.sqrt(plain_sq) + epsilon)
    old = before[...]
    slab_out[...] = by_row(old - learn_rate * (direction + decay_rate * old), heads).astype(bf16)
    new_first[...] = moment
    new_second[...] = rot_sq
    new_plain[...] = plain_sq


def row_copies(slabs, out, sems, core):
    chips, rows = len(slabs), slabs[0].shape[0]
    copies = []
    for k, slab in enumerate(slabs):
        chip = sender_chip(place_of()[0], k, chips)
        copies.append(pltpu.make_async_copy(slab, out.at[pl.ds((2 * chip + core) * rows, rows)], sems.at[k]))
    for copy in copies:
        copy.start()
    return copies


def place_own_kernel(chips, *refs):
    slabs, state, (out, *rest) = refs[:chips], refs[chips : chips + 3], refs[chips + 3 :]
    new_state, stages, sems = rest[:3], rest[3:6], rest[6]
    copies = row_copies(slabs, out, sems, place_of()[1])
    for i, (held, stage, new) in enumerate(zip(state, stages, new_state)):
        stage[...] = by_row(held[...], new.shape[1])
        copies.append(pltpu.make_async_copy(stage, new, sems.at[chips + i]))
        copies[-1].start()
    for copy in copies:
        copy.wait()


def place_rest_kernel(chips, *refs):
    slabs, shares, (out, grad_latent, total, sems) = refs[1 : 1 + chips], refs[1 + chips : -4], refs[-4:]
    copies = row_copies(slabs, out, sems, 1 - place_of()[1])
    total[...] = functools.reduce(jnp.add, [x[...].astype(f32) for x in shares]).astype(bf16)
    last = pltpu.make_async_copy(total, grad_latent, sems.at[chips])
    last.start()
    for copy in copies + [last]:
        copy.wait()


def local(latent, q_nope, q_rope, k_rope, grad_out, offsets, weight, basis, first_moment, second_rot, second_plain):
    seq_len, latent_dim = latent.shape
    width, heads, _ = weight.shape
    dp, parts = lax.axis_size("dp"), lax.axis_size("tensor")
    chips = dp // 2
    rows = width // dp
    part_rows = seq_len // parts
    rope_dim = k_rope.shape[1]

    def core_swap(x):
        return lax.ppermute(x, "dp", [(i, i ^ 1) for i in range(dp)])

    def chip_move(x, k):
        if chips & (chips - 1):
            pairs = [(i, (i + 2 * k) % dp) for i in range(dp)]
        else:
            pairs = [(i, i ^ (2 * k)) for i in range(dp)]
        return lax.ppermute(x, "dp", pairs)

    def part_move(x, s):
        return lax.ppermute(x, "tensor", [(i, (i + s) % parts) for i in range(parts)])

    piece = (heads, rows, latent_dim)
    state = (rows, heads, latent_dim)
    send, keep, grad_kv, wall, own_weight = pl.pallas_call(
        attend_kernel,
        out_shape=(
            pltpu.VMEM((chips,) + piece, bf16),
            pltpu.VMEM((chips,) + piece, bf16),
            pltpu.VMEM((seq_len, heads * width), bf16),
            pltpu.VMEM((heads * width, latent_dim), bf16),
            pltpu.VMEM(state, bf16),
        ),
        in_specs=[in_vmem] + [in_hbm] * 6,
        out_specs=(in_vmem,) * 5,
        scratch_shapes=[
            pltpu.VMEM(latent.shape, bf16),
            pltpu.VMEM(q_nope.shape, bf16),
            pltpu.VMEM(q_rope.shape, bf16),
            pltpu.VMEM((rope_dim, seq_len), bf16),
            pltpu.VMEM(grad_out.shape, bf16),
            pltpu.VMEM(weight.shape, bf16),
            pltpu.VMEM((seq_len, seq_len), f32),
            pltpu.VMEM((heads, dp, rows, latent_dim), bf16),
            pltpu.SemaphoreType.DMA((6,)),
        ],
        compiler_params=limit_mib(32),
        cost_estimate=pl.CostEstimate(
            flops=12 * seq_len * heads * width * latent_dim, bytes_accessed=32 * 1024 * 1024, transcendentals=0
        ),
        name="attend",
    )(jnp.broadcast_to(offsets, (8, 128)), *[
        pltpu.with_memory_space_constraint(x, pltpu.HBM)
        for x in (
            latent, q_nope, q_rope, k_rope.T, grad_out, weight
        )
    ])

    send, basis, first_moment, second_rot, second_plain = lax.optimization_barrier(
        (send, basis, first_moment, second_rot, second_plain)
    )
    came = core_swap(send)
    glat = pl.pallas_call(
        latent_kernel,
        out_shape=[pltpu.VMEM((part_rows, latent_dim), bf16)] * parts,
        in_specs=[in_vmem] * 2,
        out_specs=[in_vmem] * parts,
        scratch_shapes=[pltpu.VMEM((parts, part_rows, latent_dim), bf16)],
        compiler_params=limit_mib(8),
        name="latent_share",
    )(grad_kv, wall)
    sums = pl.pallas_call(
        pair_kernel,
        out_shape=[pltpu.VMEM(piece, f32 if k == 0 else bf16) for k in range(chips)],
        in_specs=[in_vmem] * 2,
        out_specs=[in_vmem] * chips,
        compiler_params=limit_mib(4),
        name="pair_sum",
    )(keep, came)
    sums, glat = lax.optimization_barrier((sums, glat))
    got = [sums[0]] + [chip_move(sums[k], k) for k in range(1, chips)]
    glat = [glat[0]] + [part_move(glat[s], s) for s in range(1, parts)]

    flat = (heads * rows, latent_dim)
    ready = pl.pallas_call(
        ready_kernel,
        out_shape=[pltpu.VMEM(flat, f32), pltpu.VMEM(basis.shape, bf16)] + [pltpu.VMEM(flat, f32)] * 3,
        in_specs=[in_vmem] * 5,
        out_specs=[in_vmem] * 5,
        compiler_params=limit_mib(8),
        name="ready",
    )(own_weight, basis, first_moment, second_rot, second_plain)
    new_slab, new_first, new_second, new_plain = pl.pallas_call(
        soap_kernel,
        out_shape=(pltpu.VMEM(state, bf16),) + (pltpu.VMEM(flat, f32),) * 3,
        in_specs=[in_vmem] * (5 + chips),
        out_specs=(in_vmem,) * 4,
        compiler_params=limit_mib(8),
        name="soap",
    )(*ready, *got)

    mine = [new_slab] + [chip_move(new_slab, k) for k in range(1, chips)]
    others = [core_swap(x) for x in mine]
    new_weight, new_first, new_second, new_plain = pl.pallas_call(
        functools.partial(place_own_kernel, chips),
        out_shape=(pltpu.HBM((width, heads, latent_dim), bf16),) + (pltpu.HBM(state, f32),) * 3,
        in_specs=[in_vmem] * (chips + 3),
        out_specs=(in_hbm,) * 4,
        scratch_shapes=[pltpu.VMEM(state, f32)] * 3 + [pltpu.SemaphoreType.DMA((chips + 3,))],
        compiler_params=limit_mib(4),
        name="place_own",
    )(*mine, new_first, new_second, new_plain)
    new_weight, grad_latent = pl.pallas_call(
        functools.partial(place_rest_kernel, chips),
        out_shape=(pltpu.HBM((width, heads, latent_dim), bf16), pltpu.HBM((part_rows, latent_dim), bf16)),
        in_specs=[in_hbm] + [in_vmem] * (chips + parts),
        out_specs=(in_hbm, in_hbm),
        scratch_shapes=[pltpu.VMEM((part_rows, latent_dim), bf16), pltpu.SemaphoreType.DMA((chips + 1,))],
        input_output_aliases={0: 0},
        compiler_params=limit_mib(4),
        name="place_rest",
    )(new_weight, *others, *glat)
    return (grad_latent, new_weight, new_first, new_second, new_plain)


def solution(mesh):
    state = P("dp", "tensor", None)
    return jax.shard_map(
        local,
        mesh=mesh,
        in_specs=(
            P("dp", None),
            P("dp", "tensor"),
            P("dp", "tensor"),
            P("dp", None),
            P("dp", "tensor"),
            P("dp"),
            P(None, "tensor", None),
            P(),
            state,
            state,
            state,
        ),
        out_specs=(P(("dp", "tensor"), None), P(None, "tensor", None), state, state, state),
        check_vma=False,
    )
```
